256 devices in a mesh: in: 4 (over y_hi, core), out: 8 (over y_lo, x), depth: 8 (over z).
Axes of the slice: x: 4, y: 4 (y_hi: 2, y_lo: 2; y = y_hi * 2 + y_lo), z: 8, core: 2. Of those that a mesh axis runs over, the one named last changes fastest.
Arguments:
- inputs: bfloat16 [4096, 6144], P(('depth', 'out'), 'in'), may hold values from -6 to 6
- weight: bfloat16 [6144, 24576], P(('in', 'depth'), 'out'), may hold values from -0.078125 to 0.078125
- cotangent: bfloat16 [4096, 24576], P(('depth', 'in'), 'out'), may hold values from -6 to 6
Outputs:
- activated: bfloat16 [4096, 24576], P(('depth', 'in'), 'out')
- grad_inputs: bfloat16 [4096, 6144], P(('depth', 'out'), 'in')
- grad_weight: bfloat16 [6144, 24576], P(('in', 'depth'), 'out')
The draws below stay inside these ranges and needn't reach their ends.
All inputs are finite; a program needn't handle non-finite values.
Results may differ from the reference program's by a relative error of at most 0.005.
Values may be sent and summed in bfloat16 or wider, within the bound.
No kernel may reach another device: no remote copies, remote signals or barrier semaphores. Data moves between devices by JAX's collectives and lax.ppermute only.
A program may use at most 128 MiB of HBM per device.

```python
import math
import jax
import jax.numpy as jnp
from jax import lax

D = 6144
F = 24576
TOKENS = 4096


def block_levels(own_key, extent, shards, low, largest):
    def one(axis_at, shards_of):
        draws = jax.random.uniform(jax.random.fold_in(jax.random.fold_in(own_key, 6), axis_at), (shards_of,), jnp.float32, low / len(shards), largest / len(shards))
        return jnp.repeat(jnp.exp(draws), extent[axis_at] // shards_of).reshape((-1,) + (1,) * (len(extent) - axis_at - 1))

    level = one(*shards[0])
    for cut in shards[1:]:
        level = level * one(*cut)
    return level


def scatter_about(key, dims, width, bound, split=(), kind=jnp.bfloat16):
    values = jax.random.normal(key, dims, jnp.float32) * width
    if len(split) > 0:
        values = block_levels(key, dims, split, -0.22, 0.18) * values
    return jnp.clip(values, min=-bound, max=bound).astype(kind)


def setup_inputs(seed: int = 0) -> dict:
    keys = jax.random.split(jax.random.key(seed), 4)
    return {
        "inputs": scatter_about(keys[0], (TOKENS, D), 1.0, 6.0, ((0, 64), (1, 4))),
        "weight": scatter_about(keys[1], (D, F), D ** -0.5, 0.078125, ((0, 32), (1, 8))),
        "cotangent": scatter_about(keys[2], (TOKENS, F), 1.0, 6.0, ((0, 32), (1, 8))),
    }


slope_c = math.sqrt(2.0 / math.pi)

def gelu_tanh(value):
    inner = slope_c * (value + 0.044715 * value * value * value)
    return 0.5 * value * (1.0 + jnp.tanh(inner))

def gelu_slope(value):
    inner = slope_c * (value + 0.044715 * value * value * value)
    tangent = jnp.tanh(inner)
    return 0.5 * (1.0 + tangent) + 0.5 * value * (1.0 - tangent * tangent) * slope_c * (1.0 + 3.0 * 0.044715 * value * value)

def reference(inputs, weight, cotangent):
    pre_act = jnp.dot(inputs, weight, preferred_element_type=jnp.float32)
    activated = gelu_tanh(pre_act).astype(jnp.bfloat16)
    d_hidden = (cotangent.astype(jnp.float32) * gelu_slope(pre_act)).astype(jnp.bfloat16)
    grad_inputs = lax.dot_general(d_hidden, weight, (((1,), (1,)), ((), ())), preferred_element_type=jnp.float32).astype(jnp.bfloat16)
    grad_weight = lax.dot_general(inputs, d_hidden, (((0,), (0,)), ((), ())), preferred_element_type=jnp.float32).astype(jnp.bfloat16)
    return (activated, grad_inputs, grad_weight)
```

```python
import math

import jax
import jax.numpy as jnp
from jax import lax
from jax.sharding import PartitionSpec as P

slope_c = math.sqrt(2.0 / math.pi)
CHUNKS = 4


def gelu_both(value):
    inner = slope_c * (value + 0.044715 * value * value * value)
    t = jnp.tanh(inner)
    act = 0.5 * value * (1.0 + t)
    slope = 0.5 * (1.0 + t) + 0.5 * value * (1.0 - t * t) * slope_c * (
        1.0 + 3.0 * 0.044715 * value * value
    )
    return act, slope


def mm(a, b):
    return jnp.dot(a, b, preferred_element_type=jnp.float32)


def body(inputs, weight, cotangent):
    nz = lax.axis_size("depth")
    z = lax.axis_index("depth")
    i = lax.axis_index("in")
    up = [(s, (s + 1) % nz) for s in range(nz)]
    down = [(s, (s - 1) % nz) for s in range(nz)]
    core = [(s, s ^ 1) for s in range(4)]
    yhi = [(s, s ^ 2) for s in range(4)]
    send = lax.ppermute

    wr = weight.shape[0]
    half = wr // 2
    fc = weight.shape[1] // CHUNKS
    rows = cotangent.shape[0]

    doubled = jnp.concatenate([inputs, inputs], axis=1)
    x_local = lax.dynamic_slice_in_dim(doubled, z * wr, inputs.shape[1], axis=1)
    x_group = lax.all_gather(x_local, "out", axis=0, tiled=True)
    blocks = [lax.dynamic_slice_in_dim(x_group, (i ^ k) * rows, rows, axis=0) for k in (0, 2, 1, 3)]
    x = jnp.concatenate(blocks, axis=0)
    xt = lax.optimization_barrier(x.T)

    grad_in = None
    acts, grads = [], []
    for c in range(CHUNKS):
        cols = slice(c * fc, (c + 1) * fc)
        own = weight[:, cols]
        u1, d1 = send(own, "depth", up), send(own, "depth", down)
        u2, d2 = send(u1, "depth", up), send(d1, "depth", down)
        u3, d3 = send(u2, "depth", up), send(d2, "depth", down)
        u4, d4 = send(u3[:half], "depth", up), send(d3[half:], "depth", down)
        w = jnp.concatenate([own, d1, d2, d3, u4, d4, u3, u2, u1], axis=0)
        pre = mm(x, w)
        pre = pre[: 2 * rows] + send(pre[2 * rows :], "in", core)
        pre = pre[:rows] + send(pre[rows:], "in", yhi)
        act, slope = gelu_both(pre)
        acts.append(act.astype(jnp.bfloat16))
        dh = (cotangent[:, cols].astype(jnp.float32) * slope).astype(jnp.bfloat16)
        dh = jnp.concatenate([dh, send(dh, "in", yhi)], axis=0)
        dh = jnp.concatenate([dh, send(dh, "in", core)], axis=0)
        gi = lax.dot_general(dh, w, (((1,), (1,)), ((), ())), preferred_element_type=jnp.float32)
        grad_in = gi if grad_in is None else grad_in + gi

        def part(k, dh=dh):
            return mm(xt[k * wr : (k + 1) * wr], dh)

        b16 = jnp.bfloat16
        far = part(4).astype(b16)
        u, d = send(far[:half], "depth", up), send(far[half:], "depth", down)
        pu, pd = part(3), part(5)
        u = jnp.concatenate([pu[:half] + u, pu[half:]], axis=0).astype(b16)
        d = jnp.concatenate([pd[:half], pd[half:] + d], axis=0).astype(b16)
        u, d = send(u, "depth", up), send(d, "depth", down)
        u, d = (part(2) + u).astype(b16), (part(6) + d).astype(b16)
        u, d = send(u, "depth", up), send(d, "depth", down)
        u, d = (part(1) + u).astype(b16), (part(7) + d).astype(b16)
        u, d = send(u, "depth", up), send(d, "depth", down)
        grads.append((part(0) + u + d).astype(b16))

    order = jnp.stack([grad_in[k * rows : (k + 1) * rows] for k in (0, 2, 1, 3)])
    natural = jnp.concatenate(
        [lax.dynamic_index_in_dim(order, k ^ i, axis=0, keepdims=False) for k in range(4)], axis=0
    )
    g = lax.psum_scatter(natural, "out", scatter_dimension=0, tiled=True)
    g = jnp.concatenate([g, g], axis=1)
    g = lax.dynamic_slice_in_dim(g, (nz - z) % nz * wr, inputs.shape[1], axis=1)
    return (
        jnp.concatenate(acts, axis=1),
        g.astype(jnp.bfloat16),
        jnp.concatenate(grads, axis=1),
    )


def solution(mesh):
    in_specs = (P(("depth", "out"), "in"), P(("in", "depth"), "out"), P(("depth", "in"), "out"))
    out_specs = (P(("depth", "in"), "out"), P(("depth", "out"), "in"), P(("in", "depth"), "out"))
    return jax.shard_map(body, mesh=mesh, in_specs=in_specs, out_specs=out_specs, check_vma=False)
```

```python
import math

import jax
import jax.numpy as jnp
from jax import lax
from jax.sharding import PartitionSpec as P

slope_c = math.sqrt(2.0 / math.pi)
WIDTHS = (1536, 1536)
bf16 = jnp.bfloat16


def gelu_both(value):
    inner = slope_c * (value + 0.044715 * value * value * value)
    t = jnp.tanh(inner)
    act = 0.5 * value * (1.0 + t)
    slope = 0.5 * (1.0 + t) + 0.5 * value * (1.0 - t * t) * slope_c * (
        1.0 + 3.0 * 0.044715 * value * value
    )
    return act, slope


def mm(a, b):
    return jnp.dot(a, b, preferred_element_type=jnp.float32)


def tie(value, *earlier):
    return lax.optimization_barrier((value, *earlier))[0] if earlier else value


def body(inputs, weight, cotangent):
    nz = lax.axis_size("depth")
    z = lax.axis_index("depth")
    i = lax.axis_index("in")
    up = [(s, (s + 1) % nz) for s in range(nz)]
    down = [(s, (s - 1) % nz) for s in range(nz)]
    core = [(s, s ^ 1) for s in range(4)]
    yhi = [(s, s ^ 2) for s in range(4)]

    def send(value, axis, pairs, name):
        with jax.named_scope(name):
            return lax.ppermute(value, axis, pairs)

    wr = weight.shape[0]
    half = wr // 2
    rows = cotangent.shape[0]
    cols = [slice(0, WIDTHS[0]), slice(WIDTHS[0], WIDTHS[0] + WIDTHS[1])]

    o = lax.axis_index("out")
    nx = 4
    right = [(s, s // nx * nx + (s + 1) % nx) for s in range(2 * nx)]
    left = [(s, s // nx * nx + (s - 1) % nx) for s in range(2 * nx)]
    ylo = [(s, (s + nx) % (2 * nx)) for s in range(2 * nx)]

    def at(k):
        return lax.rem(z + k, nz)

    def token_block(dx, other):
        mate = lax.rem(o // nx + other, 2) * nx + lax.rem(lax.rem(o, nx) + nx + dx, nx)
        k = i ^ (mate // 2)
        return 2 * (2 * (k % 2) + k // 2) + mate % 2

    def gather_x(later):
        tr = inputs.shape[0]
        pair = jnp.stack([inputs, send(inputs, "out", ylo, "x_ylo")])
        u, d = send(pair, "out", right, "x_r1"), send(pair, "out", left, "x_l1")
        u, d = tie(u, later), tie(d, later)
        fu, fd = send(u[0], "out", right, "x_r2"), send(d[1], "out", left, "x_l2")
        whole = jnp.zeros((2 * nx, tr, inputs.shape[1]), bf16)
        for dx, other, block in (
            (0, 0, pair[0]),
            (0, 1, pair[1]),
            (-1, 0, u[0]),
            (-1, 1, u[1]),
            (1, 0, d[0]),
            (1, 1, d[1]),
            (-2, 0, fu),
            (2, 1, fd),
        ):
            whole = lax.dynamic_update_index_in_dim(whole, block, token_block(dx, other), 0)
        return whole.reshape(2 * nx * tr, -1)

    def sum_out(g):
        g = g.reshape(2 * nx, inputs.shape[0], -1)

        def block(dx, other):
            return lax.dynamic_index_in_dim(g, token_block(dx, other), 0, keepdims=False)

        u = send(block(2, 0).astype(bf16), "out", right, "g_r1")
        d = send(block(-2, 1).astype(bf16), "out", left, "g_l1")
        u = jnp.stack([block(1, 0) + u, block(1, 1)]).astype(bf16)
        d = jnp.stack([block(-1, 0), block(-1, 1) + d]).astype(bf16)
        u, d = send(u, "out", right, "g_r2"), send(d, "out", left, "g_l2")
        own = block(0, 0) + u[0] + d[0]
        other = block(0, 1) + u[1] + d[1]
        return own + send(other.astype(bf16), "out", ylo, "g_ylo")

    def gather(own):
        w = lax.dynamic_update_index_in_dim(jnp.zeros((nz, wr, own.shape[1]), bf16), own, z, 0)
        u = d = own
        got = []
        for hop in range(1, 5):
            if hop == 4:
                u, d = u[:half], d[half:]
            u = send(u, "depth", up, f"gather_u{hop}")
            d = send(d, "depth", down, f"gather_d{hop}")
            w = lax.dynamic_update_slice(w, u[None], (at(nz - hop), 0, 0))
            w = lax.dynamic_update_slice(w, d[None], (at(hop), half if hop == 4 else 0, 0))
            got.append(u)
        return w.reshape(nz * wr, -1), got

    def sum_in(pre, name):
        both = pre[: 2 * rows] + send(pre[2 * rows :], "in", core, f"{name}_core")
        return both, lambda: both[:rows] + send(both[rows:].astype(bf16), "in", yhi, f"{name}_yhi")

    def hidden(pre, ct):
        act, slope = gelu_both(pre)
        return act.astype(bf16), (ct.astype(jnp.float32) * slope).astype(bf16)

    def gather_in(dh, name):
        dh = jnp.concatenate([dh, send(dh, "in", yhi, f"{name}_yhi")], axis=0)
        return jnp.concatenate([dh, send(dh, "in", core, f"{name}_core")], axis=0)

    def back(dh, w):
        return lax.dot_general(dh, w, (((1,), (1,)), ((), ())), preferred_element_type=jnp.float32)

    def sum_z(dh, name, beside):
        far = mm(lax.dynamic_index_in_dim(xt.reshape(nz, wr, -1), at(4), 0, keepdims=False), dh).astype(bf16)
        u = send(far[:half], "depth", up, f"{name}_u1")
        d = send(far[half:], "depth", down, f"{name}_d1")
        parts = mm(xt, tie(dh, far)).reshape(nz, wr, -1)
        work = beside(far)

        def part(k, lo=0, n=wr):
            return lax.dynamic_slice(parts, (at(k), lo, 0), (1, n, parts.shape[2]))[0]

        for hop in range(2, 5):
            if hop == 2:
                u = jnp.concatenate([part(3, 0, half) + u, part(3, half, half)], axis=0)
                d = jnp.concatenate([part(5, 0, half), part(5, half, half) + d], axis=0)
            else:
                u, d = part(5 - hop) + u, part(3 + hop) + d
            u, d = u.astype(bf16), d.astype(bf16)
            u, d = tie(u, d, *work[hop - 2]), tie(d, u, *work[hop - 2])
            u = send(u, "depth", up, f"{name}_u{hop}")
            d = send(d, "depth", down, f"{name}_d{hop}")
        return (part(0) + u + d).astype(bf16), work

    w0, got = gather(weight[:, cols[0]])
    x = gather_x(got[1])
    xt = lax.optimization_barrier(x.T)
    w1 = lax.all_gather(tie(weight[:, cols[1]], got[2]), "depth", axis=0, tiled=True)

    _, rest = sum_in(mm(x, w0), "pre0")
    act0, dh0 = hidden(rest(), cotangent[:, cols[0]])
    dh0 = gather_in(dh0, "dh0")
    p0 = mm(xt, dh0).astype(bf16)
    gw0 = lax.psum_scatter(p0, "depth", scatter_dimension=0, tiled=True)

    both, rest = sum_in(mm(tie(x, p0), w1), "pre1")
    gi = back(tie(dh0, both), w0)
    act1, dh1 = hidden(rest(), cotangent[:, cols[1]])
    dh1 = gather_in(tie(dh1, gi), "dh1")
    ring = 1024

    def beside(far):
        g = gi + back(tie(dh1, far), w1)
        p2 = mm(xt, tie(dh1[:, ring:], far)).astype(bf16)
        return (g,), (p2,), ()

    gw1, ((g,), (p2,), _) = sum_z(dh1[:, :ring], "sum1", beside)
    gw2 = lax.psum_scatter(p2, "depth", scatter_dimension=0, tiled=True)
    g = sum_out(g)
    return (
        jnp.concatenate([act0, act1], axis=1),
        g.astype(bf16),
        jnp.concatenate([gw0, gw1, gw2], axis=1),
    )


def solution(mesh):
    in_specs = (P(("depth", "out"), "in"), P(("in", "depth"), "out"), P(("depth", "in"), "out"))
    out_specs = (P(("depth", "in"), "out"), P(("depth", "out"), "in"), P(("in", "depth"), "out"))
    return jax.shard_map(body, mesh=mesh, in_specs=in_specs, out_specs=out_specs, check_vma=False)
```

```python
import math

import jax
import jax.numpy as jnp
from jax import lax
from jax.sharding import PartitionSpec as P

slope_c = math.sqrt(2.0 / math.pi)
WIDTHS = (1536, 1536)
bf16 = jnp.bfloat16


def gelu_both(value):
    inner = slope_c * (value + 0.044715 * value * value * value)
    t = jnp.tanh(inner)
    act = 0.5 * value * (1.0 + t)
    slope = 0.5 * (1.0 + t) + 0.5 * value * (1.0 - t * t) * slope_c * (
        1.0 + 3.0 * 0.044715 * value * value
    )
    return act, slope


def mm(a, b):
    return jnp.dot(a, b, preferred_element_type=jnp.float32)


def tie(value, *earlier):
    return lax.optimization_barrier((value, *earlier))[0] if earlier else value


def body(inputs, weight, cotangent):
    nz = lax.axis_size("depth")
    z = lax.axis_index("depth")
    i = lax.axis_index("in")
    up = [(s, (s + 1) % nz) for s in range(nz)]
    down = [(s, (s - 1) % nz) for s in range(nz)]
    core = [(s, s ^ 1) for s in range(4)]
    yhi = [(s, s ^ 2) for s in range(4)]

    def send(value, axis, pairs, name):
        with jax.named_scope(name):
            return lax.ppermute(value, axis, pairs)

    wr = weight.shape[0]
    half = wr // 2
    rows = cotangent.shape[0]
    cols = [slice(0, WIDTHS[0]), slice(WIDTHS[0], WIDTHS[0] + WIDTHS[1])]

    o = lax.axis_index("out")
    nx = 4
    right = [(s, s // nx * nx + (s + 1) % nx) for s in range(2 * nx)]
    left = [(s, s // nx * nx + (s - 1) % nx) for s in range(2 * nx)]
    ylo = [(s, (s + nx) % (2 * nx)) for s in range(2 * nx)]

    def at(k):
        return lax.rem(z + k, nz)

    def token_block(dx, other):
        mate = lax.rem(o // nx + other, 2) * nx + lax.rem(lax.rem(o, nx) + nx + dx, nx)
        k = i ^ (mate // 2)
        return 2 * (2 * (k % 2) + k // 2) + mate % 2

    def sum_out(g):
        g = g.reshape(2 * nx, inputs.shape[0], -1)

        def block(dx, other):
            return lax.dynamic_index_in_dim(g, token_block(dx, other), 0, keepdims=False)

        u = send(block(2, 0).astype(bf16), "out", right, "g_r1")
        d = send(block(-2, 1).astype(bf16), "out", left, "g_l1")
        u = jnp.stack([block(1, 0) + u, block(1, 1)]).astype(bf16)
        d = jnp.stack([block(-1, 0), block(-1, 1) + d]).astype(bf16)
        u, d = send(u, "out", right, "g_r2"), send(d, "out", left, "g_l2")
        own = block(0, 0) + u[0] + d[0]
        other = block(0, 1) + u[1] + d[1]
        return own + send(other.astype(bf16), "out", ylo, "g_ylo")

    def gather(own):
        w = lax.dynamic_update_index_in_dim(jnp.zeros((nz, wr, own.shape[1]), bf16), own, z, 0)
        u = d = own
        got = []
        for hop in range(1, 5):
            if hop == 4:
                u, d = u[:half], d[half:]
            u = send(u, "depth", up, f"gather_u{hop}")
            d = send(d, "depth", down, f"gather_d{hop}")
            w = lax.dynamic_update_slice(w, u[None], (at(nz - hop), 0, 0))
            w = lax.dynamic_update_slice(w, d[None], (at(hop), half if hop == 4 else 0, 0))
            got.append(u)
        return w.reshape(nz * wr, -1), got

    def sum_in(pre, name):
        both = pre[: 2 * rows] + send(pre[2 * rows :], "in", core, f"{name}_core")
        return both, lambda: both[:rows] + send(both[rows:].astype(bf16), "in", yhi, f"{name}_yhi")

    def hidden(pre, ct):
        act, slope = gelu_both(pre)
        return act.astype(bf16), (ct.astype(jnp.float32) * slope).astype(bf16)

    def gather_in(dh, name):
        dh = jnp.concatenate([dh, send(dh, "in", yhi, f"{name}_yhi")], axis=0)
        return jnp.concatenate([dh, send(dh, "in", core, f"{name}_core")], axis=0)

    def back(dh, w):
        return lax.dot_general(dh, w, (((1,), (1,)), ((), ())), preferred_element_type=jnp.float32)

    def sum_z(dh, name, beside):
        far = mm(lax.dynamic_index_in_dim(xt.reshape(nz, wr, -1), at(4), 0, keepdims=False), dh).astype(bf16)
        u = send(far[:half], "depth", up, f"{name}_u1")
        d = send(far[half:], "depth", down, f"{name}_d1")
        parts = mm(xt, tie(dh, far)).reshape(nz, wr, -1)
        work = beside(far)

        def part(k, lo=0, n=wr):
            return lax.dynamic_slice(parts, (at(k), lo, 0), (1, n, parts.shape[2]))[0]

        for hop in range(2, 5):
            if hop == 2:
                u = jnp.concatenate([part(3, 0, half) + u, part(3, half, half)], axis=0)
                d = jnp.concatenate([part(5, 0, half), part(5, half, half) + d], axis=0)
            else:
                u, d = part(5 - hop) + u, part(3 + hop) + d
            u, d = u.astype(bf16), d.astype(bf16)
            u, d = tie(u, d, *work[hop - 2]), tie(d, u, *work[hop - 2])
            u = send(u, "depth", up, f"{name}_u{hop}")
            d = send(d, "depth", down, f"{name}_d{hop}")
        return (part(0) + u + d).astype(bf16), work

    x_group = lax.all_gather(inputs, "out", axis=0, tiled=True)
    w0, got = gather(weight[:, cols[0]])
    blocks = [lax.dynamic_slice_in_dim(x_group, (i ^ k) * rows, rows, axis=0) for k in (0, 2, 1, 3)]
    x = jnp.concatenate(blocks, axis=0)
    xt = lax.optimization_barrier(x.T)
    w1 = lax.all_gather(tie(weight[:, cols[1]], got[1]), "depth", axis=0, tiled=True)

    _, rest = sum_in(mm(x, w0), "pre0")
    act0, dh0 = hidden(rest(), cotangent[:, cols[0]])
    dh0 = gather_in(dh0, "dh0")
    p0 = mm(xt, dh0).astype(bf16)
    gw0 = lax.psum_scatter(p0, "depth", scatter_dimension=0, tiled=True)

    both, rest = sum_in(mm(tie(x, p0), w1), "pre1")
    gi = back(tie(dh0, both), w0)
    act1, dh1 = hidden(rest(), cotangent[:, cols[1]])
    dh1 = gather_in(tie(dh1, gi), "dh1")
    ring = 1024

    def beside(far):
        g = gi + back(tie(dh1, far), w1)
        p2 = mm(xt, tie(dh1[:, ring:], far)).astype(bf16)
        return (g,), (p2, gw0), ()

    gw1, ((g,), (p2, _), _) = sum_z(dh1[:, :ring], "sum1", beside)
    gw2 = lax.psum_scatter(p2, "depth", scatter_dimension=0, tiled=True)
    g = sum_out(g)
    return (
        jnp.concatenate([act0, act1], axis=1),
        g.astype(bf16),
        jnp.concatenate([gw0, gw1, gw2], axis=1),
    )


def solution(mesh):
    in_specs = (P(("depth", "out"), "in"), P(("in", "depth"), "out"), P(("depth", "in"), "out"))
    out_specs = (P(("depth", "in"), "out"), P(("depth", "out"), "in"), P(("in", "depth"), "out"))
    return jax.shard_map(body, mesh=mesh, in_specs=in_specs, out_specs=out_specs, check_vma=False)
```

```python
import math

import jax
import jax.numpy as jnp
from jax import lax
from jax.sharding import PartitionSpec as P

slope_c = math.sqrt(2.0 / math.pi)
WIDTHS = (1536, 1536)
bf16 = jnp.bfloat16


def gelu_both(value):
    inner = slope_c * (value + 0.044715 * value * value * value)
    t = jnp.tanh(inner)
    act = 0.5 * value * (1.0 + t)
    slope = 0.5 * (1.0 + t) + 0.5 * value * (1.0 - t * t) * slope_c * (
        1.0 + 3.0 * 0.044715 * value * value
    )
    return act, slope


def mm(a, b):
    return jnp.dot(a, b, preferred_element_type=jnp.float32)


def tie(value, *earlier):
    return lax.optimization_barrier((value, *earlier))[0] if earlier else value


def body(inputs, weight, cotangent):
    nz = lax.axis_size("depth")
    z = lax.axis_index("depth")
    i = lax.axis_index("in")
    up = [(s, (s + 1) % nz) for s in range(nz)]
    down = [(s, (s - 1) % nz) for s in range(nz)]
    core = [(s, s ^ 1) for s in range(4)]
    yhi = [(s, s ^ 2) for s in range(4)]

    def send(value, axis, pairs, name):
        with jax.named_scope(name):
            return lax.ppermute(value, axis, pairs)

    wr = weight.shape[0]
    half = wr // 2
    rows = cotangent.shape[0]
    cols = [slice(0, WIDTHS[0]), slice(WIDTHS[0], WIDTHS[0] + WIDTHS[1])]

    o = lax.axis_index("out")
    nx = 4
    right = [(s, s // nx * nx + (s + 1) % nx) for s in range(2 * nx)]
    left = [(s, s // nx * nx + (s - 1) % nx) for s in range(2 * nx)]
    ylo = [(s, (s + nx) % (2 * nx)) for s in range(2 * nx)]

    def at(k):
        return lax.rem(z + k, nz)

    def token_block(dx, other):
        mate = lax.rem(o // nx + other, 2) * nx + lax.rem(lax.rem(o, nx) + nx + dx, nx)
        k = i ^ (mate // 2)
        return 2 * (2 * (k % 2) + k // 2) + mate % 2

    def sum_out(g):
        g = g.reshape(2 * nx, inputs.shape[0], -1)

        def block(dx, other):
            return lax.dynamic_index_in_dim(g, token_block(dx, other), 0, keepdims=False)

        u = send(block(2, 0).astype(bf16), "out", right, "g_r1")
        d = send(block(-2, 1).astype(bf16), "out", left, "g_l1")
        u = jnp.stack([block(1, 0) + u, block(1, 1)]).astype(bf16)
        d = jnp.stack([block(-1, 0), block(-1, 1) + d]).astype(bf16)
        u, d = send(u, "out", right, "g_r2"), send(d, "out", left, "g_l2")
        own = block(0, 0) + u[0] + d[0]
        other = block(0, 1) + u[1] + d[1]
        return own + send(other.astype(bf16), "out", ylo, "g_ylo")

    def gather(own):
        w = lax.dynamic_update_index_in_dim(jnp.zeros((nz, wr, own.shape[1]), bf16), own, z, 0)
        u = d = own
        got = []
        for hop in range(1, 5):
            if hop == 4:
                u, d = u[:half], d[half:]
            u = send(u, "depth", up, f"gather_u{hop}")
            d = send(d, "depth", down, f"gather_d{hop}")
            w = lax.dynamic_update_slice(w, u[None], (at(nz - hop), 0, 0))
            w = lax.dynamic_update_slice(w, d[None], (at(hop), half if hop == 4 else 0, 0))
            got.append(u)
        return w.reshape(nz * wr, -1), got

    def sum_in(pre, name):
        both = pre[: 2 * rows] + send(pre[2 * rows :], "in", core, f"{name}_core")
        return both, lambda: both[:rows] + send(both[rows:].astype(bf16), "in", yhi, f"{name}_yhi")

    def hidden(pre, ct):
        act, slope = gelu_both(pre)
        return act.astype(bf16), (ct.astype(jnp.float32) * slope).astype(bf16)

    def gather_in(dh, name):
        dh = jnp.concatenate([dh, send(dh, "in", yhi, f"{name}_yhi")], axis=0)
        return jnp.concatenate([dh, send(dh, "in", core, f"{name}_core")], axis=0)

    def back(dh, w):
        return lax.dot_general(dh, w, (((1,), (1,)), ((), ())), preferred_element_type=jnp.float32)

    def sum_z(dh, name, beside):
        far = mm(lax.dynamic_index_in_dim(xt.reshape(nz, wr, -1), at(4), 0, keepdims=False), dh).astype(bf16)
        u = send(far[:half], "depth", up, f"{name}_u1")
        d = send(far[half:], "depth", down, f"{name}_d1")
        parts = mm(xt, tie(dh, far)).reshape(nz, wr, -1)
        work = beside(far)

        def part(k, lo=0, n=wr):
            return lax.dynamic_slice(parts, (at(k), lo, 0), (1, n, parts.shape[2]))[0]

        for hop in range(2, 5):
            if hop == 2:
                u = jnp.concatenate([part(3, 0, half) + u, part(3, half, half)], axis=0)
                d = jnp.concatenate([part(5, 0, half), part(5, half, half) + d], axis=0)
            else:
                u, d = part(5 - hop) + u, part(3 + hop) + d
            u, d = u.astype(bf16), d.astype(bf16)
            u, d = tie(u, d, *work[hop - 2]), tie(d, u, *work[hop - 2])
            u = send(u, "depth", up, f"{name}_u{hop}")
            d = send(d, "depth", down, f"{name}_d{hop}")
        return (part(0) + u + d).astype(bf16), work

    x_group = lax.all_gather(inputs, "out", axis=0, tiled=True)
    w0, got = gather(weight[:, cols[0]])
    blocks = [lax.dynamic_slice_in_dim(x_group, (i ^ k) * rows, rows, axis=0) for k in (0, 2, 1, 3)]
    x = jnp.concatenate(blocks, axis=0)
    xt = lax.optimization_barrier(x.T)
    w1 = lax.all_gather(tie(weight[:, cols[1]], got[1]), "depth", axis=0, tiled=True)

    _, rest = sum_in(mm(x, w0), "pre0")
    act0, dh0 = hidden(rest(), cotangent[:, cols[0]])
    dh0 = gather_in(dh0, "dh0")
    p0 = mm(xt, dh0).astype(bf16)
    gw0 = lax.psum_scatter(p0, "depth", scatter_dimension=0, tiled=True)

    both, rest = sum_in(mm(tie(x, p0), w1), "pre1")
    gi = back(tie(dh0, both), w0)
    act1, dh1 = hidden(rest(), cotangent[:, cols[1]])
    dh1 = gather_in(tie(dh1, gi), "dh1")
    ring = 1024

    def beside(far):
        g = gi + back(tie(dh1, far), w1)
        p2 = mm(xt, tie(dh1[:, ring:], far)).astype(bf16)
        return (g, p2), (gw0,), ()

    gw1, ((g, p2), _, _) = sum_z(dh1[:, :ring], "sum1", beside)
    gw2 = lax.psum_scatter(p2, "depth", scatter_dimension=0, tiled=True)
    g = sum_out(g)
    grad_weight = jnp.zeros(weight.shape, bf16)
    for value, start in ((gw0, 0), (gw2, WIDTHS[0] + ring), (gw1, WIDTHS[0])):
        grad_weight = lax.dynamic_update_slice(grad_weight, value, (0, start))
    return (
        jnp.concatenate([act0, act1], axis=1),
        g.astype(bf16),
        grad_weight,
    )


def solution(mesh):
    in_specs = (P(("depth", "out"), "in"), P(("in", "depth"), "out"), P(("depth", "in"), "out"))
    out_specs = (P(("depth", "in"), "out"), P(("depth", "out"), "in"), P(("in", "depth"), "out"))
    return jax.shard_map(body, mesh=mesh, in_specs=in_specs, out_specs=out_specs, check_vma=False)
```
